512 devices in a mesh: tm: 4 (over x), rows: 128 (over z, y, core).
Axes of the slice: x: 4, y: 8, z: 8, core: 2. Of those that a mesh axis runs over, the one named last changes fastest.
Arguments:
- frames: bfloat16 [16, 1024, 64, 128], P('tm', 'rows'), may hold values from -50 to 50
- video_pos: int32 [16], P('tm'), may hold values from 0 to 3, as said below
- norm1_gain: float32 [128], replicated, may hold values from 0.25 to 1.75
- norm1_shift: float32 [128], replicated, may hold values from -3 to 3
- conv1_weight: bfloat16 [3, 3, 3, 128, 128], replicated, may hold values from -0.109375 to 0.109375
- norm2_gain: float32 [128], replicated, may hold values from 0.25 to 1.75
- norm2_shift: float32 [128], replicated, may hold values from -3 to 3
- conv2_weight: bfloat16 [3, 3, 3, 128, 128], replicated, may hold values from -0.109375 to 0.109375
Outputs:
- encoded: bfloat16 [16, 1024, 64, 128], P('tm', 'rows')
The draws below stay inside these ranges and needn't reach their ends.
Inputs may be any that keep to these rules, and one draw needn't show every extreme that they name: video_pos[0] = 0, and each later frame's value is 0 (a new video begins) or one more than the previous frame's; a video begins only at frame 0 and at frames whose index modulo 4 is 1 or 2; no video is longer than 4 frames, and one is exactly that long.
All inputs are finite; a program needn't handle non-finite values.
Results may differ from the reference program's by a relative error of at most 0.0038.
Values may be sent and summed in bfloat16 or wider, within the bound.
A program may use at most 64 MiB of HBM per device.

```python
import jax
import jax.numpy as jnp
from jax import lax

C = 128
GROUPS = 32
T_DEV = 4
WCOL = 64
FR = 16
H = 1024


def draw_frames(key, part):
    key = jax.random.fold_in(key, 2)
    key_base, key_rows, key_chan = jax.random.split(key, 3)
    ramp = jnp.arange(H, dtype=jnp.float32) / max(H - 1, 1)
    row_scale = 3.0 ** ramp * jnp.exp(jax.random.uniform(key_rows, (H,), jnp.float32, -0.5, 0.5))
    chan_scale = jnp.exp(jax.random.uniform(key_chan, (C,), jnp.float32, -1.2, 1.1))
    base = jnp.clip(jax.random.normal(key_base, (FR, H, WCOL, C), jnp.float32), -6.0, 6.0)
    values = base * row_scale[None, :, None, None] * chan_scale[None, None, None, :] * 0.5
    return values.astype(jnp.bfloat16)


def draw_video_pos(key, part):
    key = jax.random.fold_in(key, 1)
    index = jnp.arange(FR, dtype=jnp.int32)
    residue = index % T_DEV
    allowed = (index >= T_DEV) & (residue >= 2) & (residue <= T_DEV - 2)
    random_marks = (jax.random.randint(key, (FR,), 0, 3) == 0) & allowed
    forced = (index == 0) | (residue == 1)
    marks = random_marks | forced
    starts = jnp.where(marks, index, 0)
    latest = lax.cummax(starts, axis=0)
    return (index - latest).astype(jnp.int32)


def centred(rng, extent, deviation, limit, kind=jnp.bfloat16):
    values = deviation * jax.random.normal(rng, extent, jnp.float32)
    return jnp.clip(values, min=-limit, max=limit).astype(kind)


def setup_inputs(seed: int = 0) -> dict:
    seeds = jax.random.split(jax.random.key(seed), 9)
    return {
        "frames": draw_frames(jax.random.fold_in(seeds[8], 71), 0),
        "video_pos": draw_video_pos(jax.random.fold_in(seeds[8], 71), 0),
        "norm1_gain": jnp.clip(1.0 + 0.15 * jax.random.normal(seeds[2], (C,), jnp.float32), 0.25, 1.75),
        "norm1_shift": centred(seeds[3], (C,), 0.5, 3.0, jnp.float32),
        "conv1_weight": centred(seeds[4], (3, 3, 3, C, C), (27 * C) ** -0.5, 0.109375),
        "norm2_gain": jnp.clip(1.0 + 0.15 * jax.random.normal(seeds[5], (C,), jnp.float32), 0.25, 1.75),
        "norm2_shift": centred(seeds[6], (C,), 0.5, 3.0, jnp.float32),
        "conv2_weight": centred(seeds[7], (3, 3, 3, C, C), (27 * C) ** -0.5, 0.109375),
    }


def group_stats(values, groups):
    nf, nh, nw, nc = values.shape
    split = values.reshape(nf, nh, nw, groups, nc // groups)
    return (lax.optimization_barrier(jnp.sum(split, axis=(1, 2, 4))), lax.optimization_barrier(jnp.sum(split * split, axis=(1, 2, 4))))

def normalize(values, sum_one, sum_two, count, gain, shift, groups):
    mean = sum_one / count
    spread = sum_two / count - mean * mean
    scale = lax.rsqrt(spread + 1e-06)
    repeat = values.shape[3] // groups
    mean_c = jnp.repeat(mean, repeat, axis=1)[:, None, None, :]
    scale_c = jnp.repeat(scale, repeat, axis=1)[:, None, None, :]
    normed = (values - mean_c) * scale_c * gain + shift
    return jax.nn.silu(normed).astype(jnp.bfloat16)

def tap_sources(positions, offsets):
    steps = jnp.arange(3, dtype=jnp.int32)
    back = jnp.minimum(2 - steps[None, :], positions[:, None])
    return (offsets[:, None] - back).astype(jnp.int32)

def conv_frames(padded, wmat, sources):
    out_h = padded.shape[1] - 2
    out_w = padded.shape[2] - 2

    def one_frame(src):
        pieces = []
        for tap in range(3):
            frame = lax.dynamic_index_in_dim(padded, src[tap], 0, keepdims=False)
            for row_tap in range(3):
                for col_tap in range(3):
                    pieces.append(frame[row_tap:row_tap + out_h, col_tap:col_tap + out_w])
        columns = jnp.concatenate(pieces, axis=2).reshape(out_h * out_w, -1)
        result = jnp.dot(columns, wmat, preferred_element_type=jnp.float32)
        return result.reshape(out_h, out_w, -1)
    return lax.map(one_frame, sources)

def reference(frames, video_pos, norm1_gain, norm1_shift, conv1_weight, norm2_gain, norm2_shift, conv2_weight):
    chans = frames.shape[3]
    wmat_one = conv1_weight.reshape(27 * chans, chans)
    wmat_two = conv2_weight.reshape(27 * chans, chans)
    count = frames.shape[1] * frames.shape[2] * (chans // GROUPS)
    widths = ((0, 0), (1, 1), (1, 1), (0, 0))
    values = frames.astype(jnp.float32)
    sum_one, sum_two = group_stats(values, GROUPS)
    act_one = normalize(values, sum_one, sum_two, count, norm1_gain, norm1_shift, GROUPS)
    sources = tap_sources(video_pos, jnp.arange(frames.shape[0], dtype=jnp.int32))
    middle = conv_frames(jnp.pad(act_one, widths), wmat_one, sources)
    sum_one, sum_two = group_stats(middle, GROUPS)
    act_two = normalize(middle, sum_one, sum_two, count, norm2_gain, norm2_shift, GROUPS)
    branch = conv_frames(jnp.pad(act_two, widths), wmat_two, sources)
    return (values + branch).astype(jnp.bfloat16)
```

```python
import functools

import jax
import jax.numpy as jnp
from jax import lax
from jax.experimental import pallas as pl
from jax.experimental.pallas import tpu as pltpu
from jax.sharding import PartitionSpec as P

GROUP = 4
EPS = 1e-06
MESH = pl.DeviceIdType.MESH


def near_size(rows):
    size = 1
    while size * size < rows:
        size *= 2
    return size


def kernel(
    nt,
    nr,
    frames,
    video_pos,
    gain1,
    shift1,
    weight1,
    gain2,
    shift2,
    weight2,
    out,
    ext,
    ext2,
    own2,
    mid,
    act,
    pad,
    wraw,
    wpair,
    params,
    pos,
    affine,
    stat,
    part,
    near,
    far,
    prev,
    result,
    load_sem,
    out_sem,
    send_sem,
    recv_sem,
):
    nf, hr, wc, ch = frames.shape
    pairs = hr // 2
    near_n = near.shape[1]
    far_n = far.shape[1]
    count = float(nr * hr * wc * GROUP)
    t = lax.axis_index("tm")
    r = lax.axis_index("rows")
    in_near = lax.rem(r, near_n)
    in_far = lax.div(r, near_n)
    above = lax.rem(r + nr - 1, nr)
    below = lax.rem(r + 1, nr)
    after = lax.rem(t + 1, nt)
    before = lax.rem(t + nt - 1, nt)

    def near_peer(step):
        return in_far * near_n + lax.rem(in_near + step, near_n)

    def far_peer(step):
        return lax.rem(in_far + step, far_n) * near_n + in_near

    loads = [
        pltpu.make_async_copy(frames, ext.at[2 : 2 + nf, 1 : 1 + hr], load_sem.at[0]),
        pltpu.make_async_copy(weight1, wraw.at[0], load_sem.at[1]),
        pltpu.make_async_copy(weight2, wraw.at[1], load_sem.at[2]),
        pltpu.make_async_copy(video_pos, pos, load_sem.at[3]),
        pltpu.make_async_copy(gain1, params.at[0], load_sem.at[4]),
        pltpu.make_async_copy(shift1, params.at[1], load_sem.at[5]),
        pltpu.make_async_copy(gain2, params.at[2], load_sem.at[6]),
        pltpu.make_async_copy(shift2, params.at[3], load_sem.at[7]),
    ]
    for load in loads:
        load.start()

    barrier = pltpu.get_barrier_semaphore()

    def greet(tt, rr):
        pl.semaphore_signal(barrier, inc=1, device_id=(tt, rr), device_id_type=MESH)

    @pl.loop(1, near_n)
    def _(step):
        greet(t, near_peer(step))

    @pl.loop(1, far_n)
    def _(step):
        greet(t, far_peer(step))

    greet(t, above)
    greet(t, below)
    greet(before, r)
    greet(before, above)
    greet(before, below)

    def send(src, dst, which, tt, rr):
        return pltpu.make_async_remote_copy(
            src_ref=src,
            dst_ref=dst,
            send_sem=send_sem.at[which],
            recv_sem=recv_sem.at[which],
            device_id=(tt, rr),
            device_id_type=MESH,
        )

    def sum_start(phase):
        @pl.loop(1, near_n)
        def _(step):
            send(
                stat.at[phase], near.at[phase, in_near], 2 * phase, t, near_peer(step)
            ).start()

        near[phase, in_near] = stat[phase]

    def wait_many(ref, sem):
        pltpu.make_async_copy(ref, ref, sem).wait()

    def sum_middle(phase):
        wait_many(near.at[phase, 0 : near_n - 1], recv_sem.at[2 * phase])
        total = near[phase, 0]
        for i in range(1, near_n):
            total = total + near[phase, i]
        part[phase] = total
        far[phase, in_far] = total

        @pl.loop(1, far_n)
        def _(step):
            send(
                part.at[phase], far.at[phase, in_far], 2 * phase + 1, t, far_peer(step)
            ).start()

    def sum_end(phase):
        wait_many(far.at[phase, 0 : far_n - 1], recv_sem.at[2 * phase + 1])
        total = far[phase, 0]
        for i in range(1, far_n):
            total = total + far[phase, i]
        lane = lax.broadcasted_iota(jnp.int32, total.shape, 1)
        for width in (1, 2):
            up = pltpu.roll(total, width, 1)
            down = pltpu.roll(total, ch - width, 1)
            total = total + jnp.where(lax.rem(lax.div(lane, width), 2) == 0, down, up)
        stat[2 + phase] = total

    def sum_drain(phase):
        wait_many(near.at[phase, 0 : near_n - 1], send_sem.at[2 * phase])
        wait_many(far.at[phase, 0 : far_n - 1], send_sem.at[2 * phase + 1])

    def set_affine(phase, total, first, number, at):
        mean = total[first : first + number] / count
        spread = total[nf + first : nf + first + number] / count - mean * mean
        scale = lax.rsqrt(spread + EPS) * params[2 * phase]
        affine[phase, 0, at : at + number] = scale
        affine[phase, 1, at : at + number] = params[2 * phase + 1] - mean * scale

    def fill_weights(layer):
        wp = wpair.at[layer]
        zeros = jnp.zeros((3 * ch, ch), wp.dtype)
        for k in range(3):
            for u in range(4):
                at = (4 * k + u) * 3 * ch
                for par in range(2):
                    i = u - par
                    block = wraw[layer, (3 * k + i) * 3 * ch : (3 * k + i + 1) * 3 * ch] if 0 <= i < 3 else zeros
                    wp[at : at + 3 * ch, par * ch : (par + 1) * ch] = block

    row_ok = (
        jnp.where(r > 0, 1.0, 0.0).astype(jnp.float32),
        jnp.where(r < nr - 1, 1.0, 0.0).astype(jnp.float32),
    )

    def norm_row(x, phase, s, row, slot):
        y = x * affine[phase, 0, pl.ds(s, 1)] + affine[phase, 1, pl.ds(s, 1)]
        a = y * (0.5 * jnp.tanh(0.5 * y) + 0.5)
        if row == 0:
            a = a * row_ok[0]
        if row == hr + 1:
            a = a * row_ok[1]
        pad[slot, 8 : 8 + wc] = a
        lo = (row % 2) * 3 * ch
        act[s, row // 2, :, lo : lo + ch] = pad[slot, 7 : 7 + wc].astype(act.dtype)
        act[s, row // 2, :, lo + ch : lo + 2 * ch] = a.astype(act.dtype)
        act[s, row // 2, :, lo + 2 * ch : lo + 3 * ch] = pad[slot, 9 : 9 + wc].astype(act.dtype)

    def norm_frames(phase, first, last):
        @pl.loop(first, last)
        def _(s):
            for row in range(hr + 2):
                if phase == 0:
                    x = ext[s, row].astype(jnp.float32)
                elif first < 2 or row in (0, hr + 1):
                    x = ext2[s, row].astype(jnp.float32)
                else:
                    q = row - 1
                    x = mid[s - 2, q // 2, :, (q % 2) * ch : (q % 2 + 1) * ch]
                norm_row(x, phase, s, row, row)

    def conv(layer, f):
        pieces = []
        for k in range(3):
            s = f + 2 - jnp.minimum(2 - k, pos[f])
            for half in range(2):
                pieces.append(act[s, half : half + pairs].reshape(pairs * wc, 6 * ch))
        lhs = jnp.concatenate(pieces, axis=1)
        total = jnp.dot(lhs, wpair[layer], preferred_element_type=jnp.float32)
        return total.reshape(pairs, wc, 2 * ch)

    def fold(x):
        while x.shape[0] > 1:
            half = x.shape[0] // 2
            x = x[:half] + x[half:]
        return x

    def column_sums(x):
        return jnp.sum(x, axis=0, keepdims=True)

    loads[0].wait()
    @pl.loop(0, nf)
    def _(f):
        one = jnp.zeros((8, ch), jnp.float32)
        two = jnp.zeros((8, ch), jnp.float32)
        for row in range(1, hr + 1):
            x = ext[f + 2, row].astype(jnp.float32).reshape(wc // 8, 8, ch)
            one = one + jnp.sum(x, axis=0)
            two = two + jnp.sum(x * x, axis=0)
        stat[0, pl.ds(f, 1)] = column_sums(one)
        stat[0, pl.ds(f + nf, 1)] = column_sums(two)

    pl.semaphore_wait(barrier, near_n + far_n - 2 + 5)
    sum_start(0)

    halos = [
        send(frames.at[:, hr - 1], ext.at[2 : 2 + nf, 0], 4, t, below),
        send(frames.at[:, 0], ext.at[2 : 2 + nf, hr + 1], 5, t, above),
        send(frames.at[nf - 2 : nf, hr - 1], ext.at[0:2, 0], 6, after, below),
        send(frames.at[nf - 2 : nf, 0], ext.at[0:2, hr + 1], 7, after, above),
        send(frames.at[nf - 2 : nf], ext.at[0:2, 1 : 1 + hr], 8, after, r),
    ]
    for halo in halos:
        halo.start()

    loads[1].wait()
    fill_weights(0)
    for slot in range(hr + 2):
        pad[slot, 0:8] = jnp.zeros((8, ch), jnp.float32)
        pad[slot, 8 + wc : 16 + wc] = jnp.zeros((8, ch), jnp.float32)
    sum_middle(0)
    loads[2].wait()
    fill_weights(1)
    for load in loads[3:]:
        load.wait()
    sum_end(0)
    ahead = send(stat.at[2], prev.at[0], 9, after, r)
    ahead.start()
    set_affine(0, stat[2], 0, nf, 2)
    halos[0].wait_recv()
    halos[1].wait_recv()
    norm_frames(0, 2, 2 + nf)

    def conv_one(f):
        total = conv(0, f)
        mid[f] = total
        one = jnp.sum(total.reshape(pairs * wc // 8, 8, 2 * ch), axis=0)
        two = jnp.sum((total * total).reshape(pairs * wc // 8, 8, 2 * ch), axis=0)
        one = column_sums(one[:, :ch] + one[:, ch:])
        two = column_sums(two[:, :ch] + two[:, ch:])
        stat[1, f : f + 1] = one
        stat[1, f + nf : f + nf + 1] = two
        for row in range(hr):
            if f >= nf - 2 or row in (0, hr - 1):
                own2[f, row] = total[row // 2, :, (row % 2) * ch : (row % 2 + 1) * ch].astype(own2.dtype)

    conv_one(nf - 1)
    conv_one(nf - 2)
    halos2 = [
        send(own2.at[nf - 2 : nf, hr - 1], ext2.at[0:2, 0], 10, after, below),
        send(own2.at[nf - 2 : nf, 0], ext2.at[0:2, hr + 1], 11, after, above),
        send(own2.at[nf - 2 : nf], ext2.at[0:2, 1 : 1 + hr], 12, after, r),
    ]
    for halo in halos2:
        halo.start()

    ahead.wait_recv()
    set_affine(0, prev[0], nf - 2, 2, 0)
    for halo in halos[2:]:
        halo.wait_recv()
    norm_frames(0, 0, 2)
    conv_one(0)
    conv_one(1)
    sum_start(1)
    edges2 = [
        send(own2.at[:, hr - 1], ext2.at[2 : 2 + nf, 0], 13, t, below),
        send(own2.at[:, 0], ext2.at[2 : 2 + nf, hr + 1], 14, t, above),
    ]
    for edge in edges2:
        edge.start()
    sum_middle(1)
    sum_end(1)
    ahead2 = send(stat.at[3], prev.at[1], 15, after, r)
    ahead2.start()
    set_affine(1, stat[3], 0, nf, 2)
    for edge in edges2:
        edge.wait_recv()
    norm_frames(1, 2, 2 + nf)

    def conv_two(f):
        total = conv(1, f)
        for row in range(hr):
            piece = total[row // 2, :, (row % 2) * ch : (row % 2 + 1) * ch]
            kept = ext[f + 2, row + 1].astype(jnp.float32)
            result[f, row] = (kept + piece).astype(result.dtype)
        copy = pltpu.make_async_copy(result.at[f], out.at[f], out_sem.at[f])
        copy.start()
        return copy

    copies = [conv_two(nf - 1), conv_two(nf - 2)]
    ahead2.wait_recv()
    set_affine(1, prev[1], nf - 2, 2, 0)
    for halo in halos2:
        halo.wait_recv()
    norm_frames(1, 0, 2)
    copies += [conv_two(0), conv_two(1)]
    for sent in halos + halos2 + edges2 + [ahead, ahead2]:
        sent.wait_send()
    sum_drain(0)
    sum_drain(1)
    for copy in copies:
        copy.wait()


def body(frames, video_pos, gain1, shift1, weight1, gain2, shift2, weight2):
    nt = lax.axis_size("tm")
    nr = lax.axis_size("rows")
    nf, hr, wc, ch = frames.shape
    near_n = near_size(nr)
    far_n = nr // near_n
    bf, f32 = jnp.bfloat16, jnp.float32
    hbm = pl.BlockSpec(memory_space=pl.ANY)
    call = pl.pallas_call(
        functools.partial(kernel, nt, nr),
        out_shape=jax.ShapeDtypeStruct(frames.shape, frames.dtype),
        in_specs=[hbm] * 8,
        out_specs=hbm,
        scratch_shapes=[
            pltpu.VMEM((nf + 2, hr + 2, wc, ch), bf),
            pltpu.VMEM((nf + 2, hr + 2, wc, ch), bf),
            pltpu.VMEM((nf, hr, wc, ch), bf),
            pltpu.VMEM((nf, hr // 2, wc, 2 * ch), f32),
            pltpu.VMEM((nf + 2, hr // 2 + 1, wc, 6 * ch), bf),
            pltpu.VMEM((hr + 2, wc + 16, ch), f32),
            pltpu.VMEM((2, 27 * ch, ch), bf),
            pltpu.VMEM((2, 36 * ch, 2 * ch), bf),
            pltpu.VMEM((4, 1, ch), f32),
            pltpu.SMEM((nf,), jnp.int32),
            pltpu.VMEM((2, 2, 8, ch), f32),
            pltpu.VMEM((4, 2 * nf, ch), f32),
            pltpu.VMEM((2, 2 * nf, ch), f32),
            pltpu.VMEM((2, near_n, 2 * nf, ch), f32),
            pltpu.VMEM((2, far_n, 2 * nf, ch), f32),
            pltpu.VMEM((2, 2 * nf, ch), f32),
            pltpu.VMEM((nf, hr, wc, ch), bf),
            pltpu.SemaphoreType.DMA((8,)),
            pltpu.SemaphoreType.DMA((nf,)),
            pltpu.SemaphoreType.DMA((16,)),
            pltpu.SemaphoreType.DMA((16,)),
        ],
        compiler_params=pltpu.CompilerParams(
            collective_id=0, has_side_effects=True, vmem_limit_bytes=48 * 1024 * 1024
        ),
        name="encoder_block",
    )
    return call(
        frames,
        video_pos,
        gain1.reshape(1, ch),
        shift1.reshape(1, ch),
        weight1.reshape(27 * ch, ch),
        gain2.reshape(1, ch),
        shift2.reshape(1, ch),
        weight2.reshape(27 * ch, ch),
    )


def solution(mesh):
    placed = (P("tm", "rows", None, None), P("tm"), P(), P(), P(), P(), P(), P())
    return jax.shard_map(
        body, mesh=mesh, in_specs=placed, out_specs=P("tm", "rows", None, None), check_vma=False
    )
```

```python
import functools

import jax
import jax.numpy as jnp
from jax import lax
from jax.experimental import pallas as pl
from jax.experimental.pallas import tpu as pltpu
from jax.sharding import PartitionSpec as P

GROUP = 4
EPS = 1e-06
MESH = pl.DeviceIdType.MESH


def near_size(rows):
    size = 1
    while size * size < rows:
        size *= 2
    return size


def kernel(
    nt,
    nr,
    frames,
    video_pos,
    gain1,
    shift1,
    weight1,
    gain2,
    shift2,
    weight2,
    out,
    ext,
    ext2,
    own2,
    mid,
    acc,
    act,
    pad,
    wraw,
    wpair,
    params,
    pos,
    affine,
    stat,
    packed,
    part,
    near,
    far,
    prev,
    load_sem,
    send_sem,
    recv_sem,
):
    nf, hr, wc, ch = frames.shape
    pairs = hr // 2
    near_n = near.shape[1]
    far_n = far.shape[1]
    count = float(nr * hr * wc * GROUP)
    t = lax.axis_index("tm")
    r = lax.axis_index("rows")
    in_near = lax.rem(r, near_n)
    in_far = lax.div(r, near_n)
    above = lax.rem(r + nr - 1, nr)
    below = lax.rem(r + 1, nr)
    after = lax.rem(t + 1, nt)
    before = lax.rem(t + nt - 1, nt)

    def near_peer(step):
        return in_far * near_n + lax.rem(in_near + step, near_n)

    def far_peer(step):
        return lax.rem(in_far + step, far_n) * near_n + in_near

    loads = [
        pltpu.make_async_copy(frames, ext.at[2 : 2 + nf, 1 : 1 + hr], load_sem.at[0]),
        pltpu.make_async_copy(weight1, wraw.at[0], load_sem.at[1]),
        pltpu.make_async_copy(weight2, wraw.at[1], load_sem.at[2]),
        pltpu.make_async_copy(video_pos, pos, load_sem.at[3]),
        pltpu.make_async_copy(gain1, params.at[0], load_sem.at[4]),
        pltpu.make_async_copy(shift1, params.at[1], load_sem.at[5]),
        pltpu.make_async_copy(gain2, params.at[2], load_sem.at[6]),
        pltpu.make_async_copy(shift2, params.at[3], load_sem.at[7]),
    ]
    for load in loads:
        load.start()

    barrier = pltpu.get_barrier_semaphore()

    def greet(tt, rr):
        pl.semaphore_signal(barrier, inc=1, device_id=(tt, rr), device_id_type=MESH)

    @pl.loop(1, near_n)
    def _(step):
        greet(t, near_peer(step))

    @pl.loop(1, far_n)
    def _(step):
        greet(t, far_peer(step))

    @pl.loop(0, far_n)
    def _(step):
        greet(before, far_peer(step))

    greet(t, above)
    greet(t, below)
    greet(before, above)
    greet(before, below)

    def send(src, dst, which, tt, rr):
        return pltpu.make_async_remote_copy(
            src_ref=src,
            dst_ref=dst,
            send_sem=send_sem.at[which],
            recv_sem=recv_sem.at[which],
            device_id=(tt, rr),
            device_id_type=MESH,
        )

    lane = lax.broadcasted_iota(jnp.int32, (8, ch), 1)
    own_lane = lax.rem(lane, GROUP) == lax.rem(lax.broadcasted_iota(jnp.int32, (8, ch), 0), GROUP)

    def group_sums(x):
        for width in (1, 2):
            up = pltpu.roll(x, width, 1)
            down = pltpu.roll(x, ch - width, 1)
            x = x + jnp.where(lax.rem(lax.div(lane, width), 2) == 0, down, up)
        return x

    def sum_start(phase):
        own = jnp.where(own_lane, group_sums(stat[phase]), 0.0)
        one = jnp.sum(own[:nf], axis=0, keepdims=True)
        two = jnp.sum(own[nf:], axis=0, keepdims=True)
        packed[phase] = jnp.concatenate([one, two], axis=0)
        near[phase, in_near] = packed[phase]

        @pl.loop(1, near_n)
        def _(step):
            send(
                packed.at[phase], near.at[phase, in_near], 3 * phase, t, near_peer(step)
            ).start()

    def wait_many(ref, sem):
        pltpu.make_async_copy(ref, ref, sem).wait()

    def sum_middle(phase):
        wait_many(near.at[phase, 0 : near_n - 1], recv_sem.at[3 * phase])
        total = jnp.sum(near[phase], axis=0)
        part[phase] = total
        far[phase, in_far] = total

        @pl.loop(1, far_n)
        def _(step):
            send(
                part.at[phase], far.at[phase, in_far], 3 * phase + 1, t, far_peer(step)
            ).start()

        @pl.loop(0, far_n)
        def _(step):
            send(
                part.at[phase], prev.at[phase, in_far], 3 * phase + 2, after, far_peer(step)
            ).start()

    def sum_drain(phase):
        wait_many(near.at[phase, 0 : near_n - 1], send_sem.at[3 * phase])
        wait_many(far.at[phase, 0 : far_n - 1], send_sem.at[3 * phase + 1])
        wait_many(prev.at[phase], send_sem.at[3 * phase + 2])

    def set_affine(phase, total, at):
        sums = [
            group_sums(jnp.where(own_lane, jnp.broadcast_to(total[i : i + 1], (8, ch)), 0.0))
            for i in range(2)
        ]
        mean = sums[0] / count
        spread = sums[1] / count - mean * mean
        scale = lax.rsqrt(spread + EPS) * params[2 * phase]
        affine[phase, at, 0] = scale
        affine[phase, at, 1] = params[2 * phase + 1] - mean * scale

    def own_affine(phase):
        wait_many(far.at[phase, 0 : far_n - 1], recv_sem.at[3 * phase + 1])
        set_affine(phase, jnp.sum(far[phase], axis=0), 1)

    def prev_affine(phase):
        wait_many(prev.at[phase], recv_sem.at[3 * phase + 2])
        set_affine(phase, jnp.sum(prev[phase], axis=0), 0)

    def fill_weights(layer):
        zeros = jnp.zeros((3 * ch, ch), wpair.dtype)
        for k in range(3):
            for i in range(3):
                tap = wraw[layer, (3 * k + i) * 3 * ch : (3 * k + i + 1) * 3 * ch]
                for par in range(2):
                    u = i + par
                    wpair[layer, k, u * 3 * ch : (u + 1) * 3 * ch, par * ch : (par + 1) * ch] = tap
            wpair[layer, k, 9 * ch : 12 * ch, 0:ch] = zeros
            wpair[layer, k, 0 : 3 * ch, ch : 2 * ch] = zeros

    row_ok = (
        jnp.where(r > 0, 1.0, 0.0).astype(jnp.float32),
        jnp.where(r < nr - 1, 1.0, 0.0).astype(jnp.float32),
    )

    def norm_row(x, phase, s, row, own):
        f = s - 2 if own else s + nf - 2
        slot = row
        y = x * affine[phase, int(own), 0, pl.ds(f, 1)] + affine[phase, int(own), 1, pl.ds(f, 1)]
        a = y * (0.5 * jnp.tanh(0.5 * y) + 0.5)
        if row == 0:
            a = a * row_ok[0]
        if row == hr + 1:
            a = a * row_ok[1]
        pad[slot, 8 : 8 + wc] = a
        lo = (row % 2) * 3 * ch
        act[s, row // 2, :, lo : lo + ch] = pad[slot, 7 : 7 + wc].astype(act.dtype)
        act[s, row // 2, :, lo + ch : lo + 2 * ch] = a.astype(act.dtype)
        act[s, row // 2, :, lo + 2 * ch : lo + 3 * ch] = pad[slot, 9 : 9 + wc].astype(act.dtype)

    def norm_frame(phase, s, own):
        for row in range(hr + 2):
            if phase == 0:
                x = ext[s, row].astype(jnp.float32)
            elif not own or row in (0, hr + 1):
                x = ext2[s, row].astype(jnp.float32)
            else:
                q = row - 1
                x = mid[s - 2, q // 2, :, (q % 2) * ch : (q % 2 + 1) * ch]
            norm_row(x, phase, s, row, own)

    def product(layer, s, w):
        lhs = jnp.concatenate(
            [act[s, half : half + pairs].reshape(pairs * wc, 6 * ch) for half in range(2)], axis=1
        )
        return jnp.dot(lhs, wpair[layer, w], preferred_element_type=jnp.float32)

    def source(f, k):
        return f + 2 - jnp.minimum(2 - k, pos[f])

    def conv_own(layer):
        norm_frame(layer, 5, True)
        acc[3] = product(layer, 5, 2)
        norm_frame(layer, 4, True)
        acc[3] = acc[3] + product(layer, 4, 1)
        acc[2] = product(layer, 4, 2)
        norm_frame(layer, 3, True)
        acc[1] = product(layer, 3, 2)
        norm_frame(layer, 2, True)
        acc[0] = product(layer, 2, 2)
        acc[3] = acc[3] + product(layer, source(3, 0), 0)
        acc[2] = acc[2] + product(layer, source(2, 1), 1) + product(layer, source(2, 0), 0)
        acc[1] = acc[1] + product(layer, source(1, 1), 1)

    def conv_prev(layer):
        norm_frame(layer, 1, False)
        acc[1] = acc[1] + product(layer, source(1, 0), 0)
        norm_frame(layer, 0, False)
        acc[0] = acc[0] + product(layer, source(0, 1), 1) + product(layer, source(0, 0), 0)

    def column_sums(x):
        return jnp.sum(x, axis=0, keepdims=True)

    loads[0].wait()
    @pl.loop(0, nf)
    def _(f):
        one = jnp.zeros((8, ch), jnp.float32)
        two = jnp.zeros((8, ch), jnp.float32)
        for row in range(1, hr + 1):
            x = ext[f + 2, row].astype(jnp.float32).reshape(wc // 8, 8, ch)
            one = one + jnp.sum(x, axis=0)
            two = two + jnp.sum(x * x, axis=0)
        stat[0, pl.ds(f, 1)] = column_sums(one)
        stat[0, pl.ds(f + nf, 1)] = column_sums(two)

    pl.semaphore_wait(barrier, near_n - 1 + 2 * far_n - 1 + 4)
    sum_start(0)

    halos = [
        send(frames.at[:, hr - 1], ext.at[2 : 2 + nf, 0], 6, t, below),
        send(frames.at[:, 0], ext.at[2 : 2 + nf, hr + 1], 7, t, above),
        send(frames.at[nf - 2 : nf, hr - 1], ext.at[0:2, 0], 8, after, below),
        send(frames.at[nf - 2 : nf, 0], ext.at[0:2, hr + 1], 9, after, above),
        send(frames.at[nf - 2 : nf], ext.at[0:2, 1 : 1 + hr], 10, after, r),
    ]
    for halo in halos:
        halo.start()

    loads[1].wait()
    fill_weights(0)
    for slot in range(hr + 2):
        pad[slot, 0:8] = jnp.zeros((8, ch), jnp.float32)
        pad[slot, 8 + wc : 16 + wc] = jnp.zeros((8, ch), jnp.float32)
    sum_middle(0)
    loads[2].wait()
    fill_weights(1)
    for load in loads[3:]:
        load.wait()
    own_affine(0)
    halos[0].wait_recv()
    halos[1].wait_recv()
    conv_own(0)

    def middle_done(f):
        total = acc[f].reshape(pairs, wc, 2 * ch)
        mid[f] = total
        one = jnp.sum(total.reshape(pairs * wc // 8, 8, 2 * ch), axis=0)
        two = jnp.sum((total * total).reshape(pairs * wc // 8, 8, 2 * ch), axis=0)
        one = column_sums(one[:, :ch] + one[:, ch:])
        two = column_sums(two[:, :ch] + two[:, ch:])
        stat[1, f : f + 1] = one
        stat[1, f + nf : f + nf + 1] = two
        for row in range(hr):
            if f >= nf - 2 or row in (0, hr - 1):
                own2[f, row] = total[row // 2, :, (row % 2) * ch : (row % 2 + 1) * ch].astype(own2.dtype)

    def send_middle(first):
        sends = [
            send(own2.at[nf - 2 : nf, hr - 1], ext2.at[0:2, 0], first, after, below),
            send(own2.at[nf - 2 : nf, 0], ext2.at[0:2, hr + 1], first + 1, after, above),
            send(own2.at[nf - 2 : nf], ext2.at[0:2, 1 : 1 + hr], first + 2, after, r),
        ]
        for each in sends:
            each.start()
        return sends

    middle_done(3)
    middle_done(2)
    halos2 = send_middle(11)
    prev_affine(0)
    for halo in halos[2:]:
        halo.wait_recv()
    conv_prev(0)
    for f in (1, 0):
        middle_done(f)
    sum_start(1)
    edges2 = [
        send(own2.at[:, hr - 1], ext2.at[2 : 2 + nf, 0], 17, t, below),
        send(own2.at[:, 0], ext2.at[2 : 2 + nf, hr + 1], 18, t, above),
    ]
    for edge in edges2:
        edge.start()
    sum_middle(1)
    own_affine(1)
    for edge in edges2:
        edge.wait_recv()
    conv_own(1)

    def output_done(f):
        total = acc[f].reshape(pairs, wc, 2 * ch)
        for row in range(hr):
            piece = total[row // 2, :, (row % 2) * ch : (row % 2 + 1) * ch]
            kept = ext[f + 2, row + 1].astype(jnp.float32)
            out[f, row] = (kept + piece).astype(out.dtype)

    output_done(3)
    output_done(2)
    prev_affine(1)
    for halo in halos2:
        halo.wait_recv()
    conv_prev(1)
    for f in (1, 0):
        output_done(f)
    for sent in halos + halos2 + edges2:
        sent.wait_send()
    sum_drain(0)
    sum_drain(1)

def body(frames, video_pos, gain1, shift1, weight1, gain2, shift2, weight2):
    nt = lax.axis_size("tm")
    nr = lax.axis_size("rows")
    nf, hr, wc, ch = frames.shape
    near_n = near_size(nr)
    far_n = nr // near_n
    bf, f32 = jnp.bfloat16, jnp.float32
    hbm = pl.BlockSpec(memory_space=pltpu.HBM)
    call = pl.pallas_call(
        functools.partial(kernel, nt, nr),
        out_shape=pltpu.VMEM(frames.shape, frames.dtype),
        in_specs=[hbm] * 8,
        out_specs=pl.BlockSpec(memory_space=pltpu.VMEM),
        scratch_shapes=[
            pltpu.VMEM((nf + 2, hr + 2, wc, ch), bf),
            pltpu.VMEM((nf + 2, hr + 2, wc, ch), bf),
            pltpu.VMEM((nf, hr, wc, ch), bf),
            pltpu.VMEM((nf, hr // 2, wc, 2 * ch), f32),
            pltpu.VMEM((nf, hr // 2 * wc, 2 * ch), f32),
            pltpu.VMEM((nf + 2, hr // 2 + 1, wc, 6 * ch), bf),
            pltpu.VMEM((hr + 2, wc + 16, ch), f32),
            pltpu.VMEM((2, 27 * ch, ch), bf),
            pltpu.VMEM((2, 3, 12 * ch, 2 * ch), bf),
            pltpu.VMEM((4, 1, ch), f32),
            pltpu.SMEM((nf,), jnp.int32),
            pltpu.VMEM((2, 2, 2, 8, ch), f32),
            pltpu.VMEM((2, 2 * nf, ch), f32),
            pltpu.VMEM((2, 2, ch), f32),
            pltpu.VMEM((2, 2, ch), f32),
            pltpu.VMEM((2, near_n, 2, ch), f32),
            pltpu.VMEM((2, far_n, 2, ch), f32),
            pltpu.VMEM((2, far_n, 2, ch), f32),
            pltpu.SemaphoreType.DMA((8,)),
            pltpu.SemaphoreType.DMA((19,)),
            pltpu.SemaphoreType.DMA((19,)),
        ],
        compiler_params=pltpu.CompilerParams(
            collective_id=0, has_side_effects=True, vmem_limit_bytes=40 * 1024 * 1024
        ),
        name="encoder_block",
    )
    operands = (
        frames,
        video_pos,
        gain1.reshape(1, ch),
        shift1.reshape(1, ch),
        weight1.reshape(27 * ch, ch),
        gain2.reshape(1, ch),
        shift2.reshape(1, ch),
        weight2.reshape(27 * ch, ch),
    )
    return call(*(pltpu.with_memory_space_constraint(x, pltpu.HBM) for x in operands))


def solution(mesh):
    placed = (P("tm", "rows", None, None), P("tm"), P(), P(), P(), P(), P(), P())
    return jax.shard_map(
        body, mesh=mesh, in_specs=placed, out_specs=P("tm", "rows", None, None), check_vma=False
    )
```

```python
import functools

import jax
import jax.numpy as jnp
from jax import lax
from jax.experimental import pallas as pl
from jax.experimental.pallas import tpu as pltpu
from jax.sharding import PartitionSpec as P

GROUP = 4
EPS = 1e-06
MESH = pl.DeviceIdType.MESH


def near_size(rows):
    size = 1
    while size * size < rows:
        size *= 2
    return size


def kernel(
    nt,
    nr,
    frames,
    video_pos,
    gain1,
    shift1,
    weight1,
    gain2,
    shift2,
    weight2,
    out,
    ext,
    ext2,
    own2,
    mid,
    acc,
    act,
    raw,
    turn,
    wraw,
    wpair,
    params,
    pos,
    affine,
    stat,
    packed,
    part,
    near,
    far,
    prev,
    load_sem,
    send_sem,
    recv_sem,
):
    nf, hr, wc, ch = frames.shape
    pairs = hr // 2
    near_n = near.shape[1]
    far_n = far.shape[1]
    count = float(nr * hr * wc * GROUP)
    t = lax.axis_index("tm")
    r = lax.axis_index("rows")
    in_near = lax.rem(r, near_n)
    in_far = lax.div(r, near_n)
    above = lax.rem(r + nr - 1, nr)
    below = lax.rem(r + 1, nr)
    after = lax.rem(t + 1, nt)
    before = lax.rem(t + nt - 1, nt)

    def near_peer(step):
        return in_far * near_n + lax.rem(in_near + step, near_n)

    def far_peer(step):
        return lax.rem(in_far + step, far_n) * near_n + in_near

    loads = [
        pltpu.make_async_copy(frames, ext.at[2 : 2 + nf, 1 : 1 + hr], load_sem.at[0]),
        pltpu.make_async_copy(weight1, wraw.at[0], load_sem.at[1]),
        pltpu.make_async_copy(weight2, wraw.at[1], load_sem.at[2]),
        pltpu.make_async_copy(video_pos, pos, load_sem.at[3]),
        pltpu.make_async_copy(gain1, params.at[0], load_sem.at[4]),
        pltpu.make_async_copy(shift1, params.at[1], load_sem.at[5]),
        pltpu.make_async_copy(gain2, params.at[2], load_sem.at[6]),
        pltpu.make_async_copy(shift2, params.at[3], load_sem.at[7]),
    ]
    for load in loads:
        load.start()

    barrier = pltpu.get_barrier_semaphore()

    def greet(tt, rr):
        pl.semaphore_signal(barrier, inc=1, device_id=(tt, rr), device_id_type=MESH)

    @pl.loop(1, near_n)
    def _(step):
        greet(t, near_peer(step))

    @pl.loop(1, far_n)
    def _(step):
        greet(t, far_peer(step))

    @pl.loop(0, far_n)
    def _(step):
        greet(before, far_peer(step))

    greet(t, above)
    greet(t, below)
    greet(before, above)
    greet(before, below)

    def send(src, dst, which, tt, rr):
        return pltpu.make_async_remote_copy(
            src_ref=src,
            dst_ref=dst,
            send_sem=send_sem.at[which],
            recv_sem=recv_sem.at[which],
            device_id=(tt, rr),
            device_id_type=MESH,
        )

    lane = lax.broadcasted_iota(jnp.int32, (8, ch), 1)
    own_lane = lax.rem(lane, GROUP) == lax.rem(lax.broadcasted_iota(jnp.int32, (8, ch), 0), GROUP)

    def group_sums(x):
        for width in (1, 2):
            up = pltpu.roll(x, width, 1)
            down = pltpu.roll(x, ch - width, 1)
            x = x + jnp.where(lax.rem(lax.div(lane, width), 2) == 0, down, up)
        return x

    def sum_start(phase):
        own = jnp.where(own_lane, group_sums(stat[phase]), 0.0)
        one = jnp.sum(own[:nf], axis=0, keepdims=True)
        two = jnp.sum(own[nf:], axis=0, keepdims=True)
        packed[phase] = jnp.concatenate([one, two], axis=0)
        near[phase, in_near] = packed[phase]

        @pl.loop(1, near_n)
        def _(step):
            send(
                packed.at[phase], near.at[phase, in_near], 3 * phase, t, near_peer(step)
            ).start()

    def wait_many(ref, sem):
        pltpu.make_async_copy(ref, ref, sem).wait()

    def sum_middle(phase):
        wait_many(near.at[phase, 0 : near_n - 1], recv_sem.at[3 * phase])
        total = jnp.sum(near[phase], axis=0)
        part[phase] = total
        far[phase, in_far] = total

        @pl.loop(1, far_n)
        def _(step):
            send(
                part.at[phase], far.at[phase, in_far], 3 * phase + 1, t, far_peer(step)
            ).start()

        @pl.loop(0, far_n)
        def _(step):
            send(
                part.at[phase], prev.at[phase, in_far], 3 * phase + 2, after, far_peer(step)
            ).start()

    def sum_drain(phase):
        wait_many(near.at[phase, 0 : near_n - 1], send_sem.at[3 * phase])
        wait_many(far.at[phase, 0 : far_n - 1], send_sem.at[3 * phase + 1])
        wait_many(prev.at[phase], send_sem.at[3 * phase + 2])

    def set_affine(phase, total, at):
        sums = [
            group_sums(jnp.where(own_lane, jnp.broadcast_to(total[i : i + 1], (8, ch)), 0.0))
            for i in range(2)
        ]
        mean = sums[0] / count
        spread = sums[1] / count - mean * mean
        scale = lax.rsqrt(spread + EPS) * params[2 * phase]
        affine[phase, at, 0] = scale
        affine[phase, at, 1] = params[2 * phase + 1] - mean * scale

    def own_affine(phase):
        wait_many(far.at[phase, 0 : far_n - 1], recv_sem.at[3 * phase + 1])
        set_affine(phase, jnp.sum(far[phase], axis=0), 1)

    def prev_affine(phase):
        wait_many(prev.at[phase], recv_sem.at[3 * phase + 2])
        set_affine(phase, jnp.sum(prev[phase], axis=0), 0)

    def fill_weights(layer):
        zeros = jnp.zeros((3 * ch, ch), wpair.dtype)
        for k in range(3):
            for i in range(3):
                tap = wraw[layer, (3 * k + i) * 3 * ch : (3 * k + i + 1) * 3 * ch]
                for par in range(2):
                    u = i + par
                    wpair[layer, k, u * 3 * ch : (u + 1) * 3 * ch, par * ch : (par + 1) * ch] = tap
            wpair[layer, k, 9 * ch : 12 * ch, 0:ch] = zeros
            wpair[layer, k, 0 : 3 * ch, ch : 2 * ch] = zeros

    row_ok = (
        jnp.where(r > 0, 1.0, 0.0).astype(jnp.float32),
        jnp.where(r < nr - 1, 1.0, 0.0).astype(jnp.float32),
    )

    eight = lax.broadcasted_iota(jnp.int32, (8, ch), 0)

    def norm_row(x, phase, s, row, own):
        f = s - 2 if own else s + nf - 2
        y = x * affine[phase, int(own), 0, pl.ds(f, 1)] + affine[phase, int(own), 1, pl.ds(f, 1)]
        a = y * (0.5 * jnp.tanh(0.5 * y) + 0.5)
        if row == 0:
            a = a * row_ok[0]
        if row == hr + 1:
            a = a * row_ok[1]
        first = jnp.where(eight == 0, 0.0, pltpu.roll(a[wc - 8 :], 1, 0))
        last = jnp.where(eight == 7, 0.0, pltpu.roll(a[:8], 7, 0))
        lo = (row % 2) * 3 * ch
        act[s, row // 2, :, lo : lo + ch] = jnp.concatenate([first, a[: wc - 8]], axis=0).astype(act.dtype)
        act[s, row // 2, :, lo + ch : lo + 2 * ch] = a.astype(act.dtype)
        act[s, row // 2, :, lo + 2 * ch : lo + 3 * ch] = jnp.concatenate([a[8:], last], axis=0).astype(act.dtype)

    def permute(s, rows):
        for row in rows:
            turn[row] = ext[s, row].astype(jnp.float32)
            for j in range(8):
                raw[s, row, 8 * j : 8 * j + 8] = turn[row, pl.ds(j, 8, stride=8)]

    def norm_frame(phase, s, own):
        for row in range(hr + 2):
            if phase == 0:
                x = raw[s, row]
            elif not own or row in (0, hr + 1):
                x = ext2[s, row].astype(jnp.float32)
            else:
                q = row - 1
                x = mid[s - 2, q // 2, :, (q % 2) * ch : (q % 2 + 1) * ch]
            norm_row(x, phase, s, row, own)

    def product(layer, s, w):
        lhs = jnp.concatenate(
            [act[s, half : half + pairs].reshape(pairs * wc, 6 * ch) for half in range(2)], axis=1
        )
        return jnp.dot(lhs, wpair[layer, w], preferred_element_type=jnp.float32)

    def source(f, k):
        return f + 2 - jnp.minimum(2 - k, pos[f])

    def conv_own(layer):
        norm_frame(layer, 5, True)
        acc[3] = product(layer, 5, 2)
        norm_frame(layer, 4, True)
        acc[3] = acc[3] + product(layer, 4, 1)
        acc[2] = product(layer, 4, 2)
        norm_frame(layer, 3, True)
        acc[1] = product(layer, 3, 2)
        norm_frame(layer, 2, True)
        acc[0] = product(layer, 2, 2)
        acc[3] = acc[3] + product(layer, source(3, 0), 0)
        acc[2] = acc[2] + product(layer, source(2, 1), 1) + product(layer, source(2, 0), 0)
        acc[1] = acc[1] + product(layer, source(1, 1), 1)

    def conv_prev(layer):
        norm_frame(layer, 1, False)
        acc[1] = acc[1] + product(layer, source(1, 0), 0)
        norm_frame(layer, 0, False)
        acc[0] = acc[0] + product(layer, source(0, 1), 1) + product(layer, source(0, 0), 0)

    def column_sums(x):
        return jnp.sum(x, axis=0, keepdims=True)

    loads[0].wait()
    @pl.loop(0, nf)
    def _(f):
        one = jnp.zeros((8, ch), jnp.float32)
        two = jnp.zeros((8, ch), jnp.float32)
        for row in range(1, hr + 1):
            x = ext[f + 2, row].astype(jnp.float32).reshape(wc // 8, 8, ch)
            one = one + jnp.sum(x, axis=0)
            two = two + jnp.sum(x * x, axis=0)
        stat[0, pl.ds(f, 1)] = column_sums(one)
        stat[0, pl.ds(f + nf, 1)] = column_sums(two)

    pl.semaphore_wait(barrier, near_n - 1 + 2 * far_n - 1 + 4)
    sum_start(0)

    halos = [
        send(frames.at[:, hr - 1], ext.at[2 : 2 + nf, 0], 6, t, below),
        send(frames.at[:, 0], ext.at[2 : 2 + nf, hr + 1], 7, t, above),
        send(frames.at[nf - 2 : nf, hr - 1], ext.at[0:2, 0], 8, after, below),
        send(frames.at[nf - 2 : nf, 0], ext.at[0:2, hr + 1], 9, after, above),
        send(frames.at[nf - 2 : nf], ext.at[0:2, 1 : 1 + hr], 10, after, r),
    ]
    for halo in halos:
        halo.start()

    loads[1].wait()
    fill_weights(0)

    @pl.loop(2, 2 + nf)
    def _(s):
        permute(s, range(1, 1 + hr))

    sum_middle(0)
    loads[2].wait()
    fill_weights(1)
    for load in loads[3:]:
        load.wait()
    halos[0].wait_recv()
    halos[1].wait_recv()

    @pl.loop(2, 2 + nf)
    def _(s):
        permute(s, (0, hr + 1))

    own_affine(0)
    conv_own(0)

    def middle_done(f):
        total = acc[f].reshape(pairs, wc, 2 * ch)
        mid[f] = total
        one = jnp.sum(total.reshape(pairs * wc // 8, 8, 2 * ch), axis=0)
        two = jnp.sum((total * total).reshape(pairs * wc // 8, 8, 2 * ch), axis=0)
        one = column_sums(one[:, :ch] + one[:, ch:])
        two = column_sums(two[:, :ch] + two[:, ch:])
        stat[1, f : f + 1] = one
        stat[1, f + nf : f + nf + 1] = two
        for row in range(hr):
            if f >= nf - 2 or row in (0, hr - 1):
                own2[f, row] = total[row // 2, :, (row % 2) * ch : (row % 2 + 1) * ch].astype(own2.dtype)

    def send_middle(first):
        sends = [
            send(own2.at[nf - 2 : nf, hr - 1], ext2.at[0:2, 0], first, after, below),
            send(own2.at[nf - 2 : nf, 0], ext2.at[0:2, hr + 1], first + 1, after, above),
            send(own2.at[nf - 2 : nf], ext2.at[0:2, 1 : 1 + hr], first + 2, after, r),
        ]
        for each in sends:
            each.start()
        return sends

    middle_done(3)
    middle_done(2)
    halos2 = send_middle(11)
    prev_affine(0)
    for halo in halos[2:]:
        halo.wait_recv()

    @pl.loop(0, 2)
    def _(s):
        permute(s, range(hr + 2))

    conv_prev(0)
    for f in (1, 0):
        middle_done(f)
    sum_start(1)
    edges2 = [
        send(own2.at[:, hr - 1], ext2.at[2 : 2 + nf, 0], 17, t, below),
        send(own2.at[:, 0], ext2.at[2 : 2 + nf, hr + 1], 18, t, above),
    ]
    for edge in edges2:
        edge.start()
    sum_middle(1)
    own_affine(1)
    for edge in edges2:
        edge.wait_recv()
    conv_own(1)

    def output_done(f):
        total = acc[f].reshape(pairs, wc, 2 * ch)
        for row in range(hr):
            piece = total[row // 2, :, (row % 2) * ch : (row % 2 + 1) * ch]
            for j in range(8):
                turn[row, pl.ds(j, 8, stride=8)] = piece[8 * j : 8 * j + 8]
            kept = ext[f + 2, row + 1].astype(jnp.float32)
            out[f, row] = (kept + turn[row]).astype(out.dtype)

    output_done(3)
    output_done(2)
    prev_affine(1)
    for halo in halos2:
        halo.wait_recv()
    conv_prev(1)
    for f in (1, 0):
        output_done(f)
    for sent in halos + halos2 + edges2:
        sent.wait_send()
    sum_drain(0)
    sum_drain(1)

def body(frames, video_pos, gain1, shift1, weight1, gain2, shift2, weight2):
    nt = lax.axis_size("tm")
    nr = lax.axis_size("rows")
    nf, hr, wc, ch = frames.shape
    near_n = near_size(nr)
    far_n = nr // near_n
    bf, f32 = jnp.bfloat16, jnp.float32
    hbm = pl.BlockSpec(memory_space=pltpu.HBM)
    call = pl.pallas_call(
        functools.partial(kernel, nt, nr),
        out_shape=pltpu.VMEM(frames.shape, frames.dtype),
        in_specs=[hbm] * 8,
        out_specs=pl.BlockSpec(memory_space=pltpu.VMEM),
        scratch_shapes=[
            pltpu.VMEM((nf + 2, hr + 2, wc, ch), bf),
            pltpu.VMEM((nf + 2, hr + 2, wc, ch), bf),
            pltpu.VMEM((nf, hr, wc, ch), bf),
            pltpu.VMEM((nf, hr // 2, wc, 2 * ch), f32),
            pltpu.VMEM((nf, hr // 2 * wc, 2 * ch), f32),
            pltpu.VMEM((nf + 2, hr // 2 + 1, wc, 6 * ch), bf),
            pltpu.VMEM((nf + 2, hr + 2, wc, ch), f32),
            pltpu.VMEM((hr + 2, wc, ch), f32),
            pltpu.VMEM((2, 27 * ch, ch), bf),
            pltpu.VMEM((2, 3, 12 * ch, 2 * ch), bf),
            pltpu.VMEM((4, 1, ch), f32),
            pltpu.SMEM((nf,), jnp.int32),
            pltpu.VMEM((2, 2, 2, 8, ch), f32),
            pltpu.VMEM((2, 2 * nf, ch), f32),
            pltpu.VMEM((2, 2, ch), f32),
            pltpu.VMEM((2, 2, ch), f32),
            pltpu.VMEM((2, near_n, 2, ch), f32),
            pltpu.VMEM((2, far_n, 2, ch), f32),
            pltpu.VMEM((2, far_n, 2, ch), f32),
            pltpu.SemaphoreType.DMA((8,)),
            pltpu.SemaphoreType.DMA((19,)),
            pltpu.SemaphoreType.DMA((19,)),
        ],
        compiler_params=pltpu.CompilerParams(
            collective_id=0, has_side_effects=True, vmem_limit_bytes=40 * 1024 * 1024
        ),
        name="encoder_block",
    )
    operands = (
        frames,
        video_pos,
        gain1.reshape(1, ch),
        shift1.reshape(1, ch),
        weight1.reshape(27 * ch, ch),
        gain2.reshape(1, ch),
        shift2.reshape(1, ch),
        weight2.reshape(27 * ch, ch),
    )
    return call(*(pltpu.with_memory_space_constraint(x, pltpu.HBM) for x in operands))


def solution(mesh):
    placed = (P("tm", "rows", None, None), P("tm"), P(), P(), P(), P(), P(), P())
    return jax.shard_map(
        body, mesh=mesh, in_specs=placed, out_specs=P("tm", "rows", None, None), check_vma=False
    )
```

```python
import functools

import jax
import jax.numpy as jnp
from jax import lax
from jax.experimental import pallas as pl
from jax.experimental.pallas import tpu as pltpu
from jax.sharding import PartitionSpec as P

GROUP = 4
EPS = 1e-06
MESH = pl.DeviceIdType.MESH


def near_size(rows):
    size = 1
    while size * size < rows:
        size *= 2
    return size


def kernel(
    nt,
    nr,
    frames,
    video_pos,
    gain1,
    shift1,
    weight1,
    gain2,
    shift2,
    weight2,
    out,
    ext,
    ext2,
    own2,
    acc,
    act,
    raw,
    turn,
    wraw,
    wpair,
    params,
    pos,
    affine,
    stat,
    packed,
    part,
    near,
    far,
    prev,
    load_sem,
    send_sem,
    recv_sem,
):
    nf, hr, wc, ch = frames.shape
    pairs = hr // 2
    near_n = near.shape[1]
    far_n = far.shape[1]
    count = float(nr * hr * wc * GROUP)
    t = lax.axis_index("tm")
    r = lax.axis_index("rows")
    in_near = lax.rem(r, near_n)
    in_far = lax.div(r, near_n)
    above = lax.rem(r + nr - 1, nr)
    below = lax.rem(r + 1, nr)
    after = lax.rem(t + 1, nt)
    before = lax.rem(t + nt - 1, nt)

    def far_first(n):
        return sorted(range(1, n), key=lambda step: -min(step, n - step))

    def near_peer(step):
        return in_far * near_n + lax.rem(in_near + step, near_n)

    def far_peer(step):
        return lax.rem(in_far + step, far_n) * near_n + in_near

    loads = [
        pltpu.make_async_copy(weight1, wraw.at[0], load_sem.at[1]),
        pltpu.make_async_copy(weight2, wraw.at[1], load_sem.at[2]),
        pltpu.make_async_copy(video_pos, pos, load_sem.at[3]),
        pltpu.make_async_copy(gain1, params.at[0], load_sem.at[4]),
        pltpu.make_async_copy(shift1, params.at[1], load_sem.at[5]),
        pltpu.make_async_copy(gain2, params.at[2], load_sem.at[6]),
        pltpu.make_async_copy(shift2, params.at[3], load_sem.at[7]),
    ]
    frame_loads = [
        pltpu.make_async_copy(frames.at[f], ext.at[f + 2, 1 : 1 + hr], load_sem.at[8 + f])
        for f in range(nf)
    ]
    for load in frame_loads + loads:
        load.start()

    barrier = pltpu.get_barrier_semaphore()

    def greet(tt, rr):
        pl.semaphore_signal(barrier, inc=1, device_id=(tt, rr), device_id_type=MESH)

    for step in far_first(far_n):
        greet(t, far_peer(step))
    for step in far_first(near_n):
        greet(t, near_peer(step))
    for step in far_first(far_n) + [0]:
        greet(before, far_peer(step))

    greet(t, above)
    greet(t, below)
    greet(before, above)
    greet(before, below)

    def send(src, dst, which, tt, rr):
        return pltpu.make_async_remote_copy(
            src_ref=src,
            dst_ref=dst,
            send_sem=send_sem.at[which],
            recv_sem=recv_sem.at[which],
            device_id=(tt, rr),
            device_id_type=MESH,
        )

    lane = lax.broadcasted_iota(jnp.int32, (8, ch), 1)
    own_lane = lax.rem(lane, GROUP) == lax.rem(lax.broadcasted_iota(jnp.int32, (8, ch), 0), GROUP)

    def group_sums(x):
        for width in (1, 2):
            up = pltpu.roll(x, width, 1)
            down = pltpu.roll(x, ch - width, 1)
            x = x + jnp.where(lax.rem(lax.div(lane, width), 2) == 0, down, up)
        return x

    def sum_start(phase):
        own = jnp.where(own_lane, group_sums(stat[phase]), 0.0)
        one = jnp.sum(own[:nf], axis=0, keepdims=True)
        two = jnp.sum(own[nf:], axis=0, keepdims=True)
        packed[phase] = jnp.concatenate([one, two], axis=0)
        near[phase, in_near] = packed[phase]

        for step in far_first(near_n):
            send(
                packed.at[phase], near.at[phase, in_near], 3 * phase, t, near_peer(step)
            ).start()

    def wait_many(ref, sem):
        pltpu.make_async_copy(ref, ref, sem).wait()

    def sum_middle(phase):
        wait_many(near.at[phase, 0 : near_n - 1], recv_sem.at[3 * phase])
        total = jnp.sum(near[phase], axis=0)
        part[phase] = total
        far[phase, in_far] = total

        for step in far_first(far_n):
            send(
                part.at[phase], far.at[phase, in_far], 3 * phase + 1, t, far_peer(step)
            ).start()

        for step in far_first(far_n) + [0]:
            send(
                part.at[phase], prev.at[phase, in_far], 3 * phase + 2, after, far_peer(step)
            ).start()

    def sum_drain(phase):
        wait_many(near.at[phase, 0 : near_n - 1], send_sem.at[3 * phase])
        wait_many(far.at[phase, 0 : far_n - 1], send_sem.at[3 * phase + 1])
        wait_many(prev.at[phase], send_sem.at[3 * phase + 2])

    def set_affine(phase, total, at):
        sums = [
            group_sums(jnp.where(own_lane, jnp.broadcast_to(total[i : i + 1], (8, ch)), 0.0))
            for i in range(2)
        ]
        mean = sums[0] / count
        spread = sums[1] / count - mean * mean
        scale = lax.rsqrt(spread + EPS) * params[2 * phase]
        affine[phase, at, 0] = scale
        affine[phase, at, 1] = params[2 * phase + 1] - mean * scale

    def own_affine(phase):
        wait_many(far.at[phase, 0 : far_n - 1], recv_sem.at[3 * phase + 1])
        set_affine(phase, jnp.sum(far[phase], axis=0), 1)

    def prev_affine(phase):
        wait_many(prev.at[phase], recv_sem.at[3 * phase + 2])
        set_affine(phase, jnp.sum(prev[phase], axis=0), 0)

    def fill_weights(layer):
        zeros = jnp.zeros((3 * ch, ch), wpair.dtype)
        for k in range(3):
            for i in range(3):
                tap = wraw[layer, (3 * k + i) * 3 * ch : (3 * k + i + 1) * 3 * ch]
                for par in range(2):
                    u = i + par
                    wpair[layer, k, u * 3 * ch : (u + 1) * 3 * ch, par * ch : (par + 1) * ch] = tap
            wpair[layer, k, 9 * ch : 12 * ch, 0:ch] = zeros
            wpair[layer, k, 0 : 3 * ch, ch : 2 * ch] = zeros

    row_ok = (
        jnp.where(r > 0, 1.0, 0.0).astype(jnp.float32),
        jnp.where(r < nr - 1, 1.0, 0.0).astype(jnp.float32),
    )

    eight = lax.broadcasted_iota(jnp.int32, (8, ch), 0)

    def norm_row(x, phase, s, row, own):
        f = s - 2 if own else s + nf - 2
        y = x * affine[phase, int(own), 0, pl.ds(f, 1)] + affine[phase, int(own), 1, pl.ds(f, 1)]
        a = y * (0.5 * jnp.tanh(0.5 * y) + 0.5)
        if row == 0:
            a = a * row_ok[0]
        if row == hr + 1:
            a = a * row_ok[1]
        first = jnp.where(eight == 0, 0.0, pltpu.roll(a[wc - 8 :], 1, 0))
        last = jnp.where(eight == 7, 0.0, pltpu.roll(a[:8], 7, 0))
        lo = (row % 2) * 3 * ch
        act[s, row // 2, :, lo : lo + ch] = jnp.concatenate([first, a[: wc - 8]], axis=0).astype(act.dtype)
        act[s, row // 2, :, lo + ch : lo + 2 * ch] = a.astype(act.dtype)
        act[s, row // 2, :, lo + 2 * ch : lo + 3 * ch] = jnp.concatenate([a[8:], last], axis=0).astype(act.dtype)

    def permute(s, rows):
        for row in rows:
            turn[row] = ext[s, row].astype(jnp.float32)
            for j in range(8):
                raw[s, row, 8 * j : 8 * j + 8] = turn[row, pl.ds(j, 8, stride=8)]

    def norm_frame(phase, s, own):
        for row in range(hr + 2):
            if phase == 0:
                x = raw[s, row]
            elif not own or row in (0, hr + 1):
                x = ext2[s, row].astype(jnp.float32)
            else:
                q = row - 1
                x = acc[s - 2, (q // 2) * wc : (q // 2 + 1) * wc, (q % 2) * ch : (q % 2 + 1) * ch]
            norm_row(x, phase, s, row, own)

    def product(layer, s, w):
        lhs = jnp.concatenate(
            [act[s, half : half + pairs].reshape(pairs * wc, 6 * ch) for half in range(2)], axis=1
        )
        return jnp.dot(lhs, wpair[layer, w], preferred_element_type=jnp.float32)

    def source(f, k):
        return f + 2 - jnp.minimum(2 - k, pos[f])

    def conv_own(layer):
        norm_frame(layer, 5, True)
        acc[3] = product(layer, 5, 2)
        norm_frame(layer, 4, True)
        acc[3] = acc[3] + product(layer, 4, 1)
        acc[2] = product(layer, 4, 2)
        norm_frame(layer, 3, True)
        acc[1] = product(layer, 3, 2)
        norm_frame(layer, 2, True)
        acc[0] = product(layer, 2, 2)
        acc[3] = acc[3] + product(layer, source(3, 0), 0)
        acc[2] = acc[2] + product(layer, source(2, 1), 1) + product(layer, source(2, 0), 0)
        acc[1] = acc[1] + product(layer, source(1, 1), 1)

    def conv_prev(layer):
        norm_frame(layer, 1, False)
        acc[1] = acc[1] + product(layer, source(1, 0), 0)
        norm_frame(layer, 0, False)
        acc[0] = acc[0] + product(layer, source(0, 1), 1) + product(layer, source(0, 0), 0)

    def column_sums(x):
        return jnp.sum(x, axis=0, keepdims=True)

    for f in range(nf):
        frame_loads[f].wait()
        one = jnp.zeros((8, ch), jnp.float32)
        two = jnp.zeros((8, ch), jnp.float32)
        for row in range(1, hr + 1):
            x = ext[f + 2, row].astype(jnp.float32).reshape(wc // 8, 8, ch)
            one = one + jnp.sum(x, axis=0)
            two = two + jnp.sum(x * x, axis=0)
        stat[0, f : f + 1] = column_sums(one)
        stat[0, f + nf : f + nf + 1] = column_sums(two)

    pl.semaphore_wait(barrier, near_n - 1 + 2 * far_n - 1 + 4)
    sum_start(0)

    halos = [
        send(frames.at[:, hr - 1], ext.at[2 : 2 + nf, 0], 6, t, below),
        send(frames.at[:, 0], ext.at[2 : 2 + nf, hr + 1], 7, t, above),
        send(frames.at[nf - 2 : nf, hr - 1], ext.at[0:2, 0], 8, after, below),
        send(frames.at[nf - 2 : nf, 0], ext.at[0:2, hr + 1], 9, after, above),
        send(frames.at[nf - 2 : nf], ext.at[0:2, 1 : 1 + hr], 10, after, r),
    ]
    for halo in halos:
        halo.start()

    loads[0].wait()
    fill_weights(0)

    @pl.loop(2, 2 + nf)
    def _(s):
        permute(s, range(1, 1 + hr))

    sum_middle(0)
    loads[1].wait()
    fill_weights(1)
    for load in loads[2:]:
        load.wait()
    halos[0].wait_recv()
    halos[1].wait_recv()

    @pl.loop(2, 2 + nf)
    def _(s):
        permute(s, (0, hr + 1))

    own_affine(0)
    conv_own(0)

    def middle_done(f):
        total = acc[f].reshape(pairs, wc, 2 * ch)
        one = jnp.sum(total.reshape(pairs * wc // 8, 8, 2 * ch), axis=0)
        two = jnp.sum((total * total).reshape(pairs * wc // 8, 8, 2 * ch), axis=0)
        one = column_sums(one[:, :ch] + one[:, ch:])
        two = column_sums(two[:, :ch] + two[:, ch:])
        stat[1, f : f + 1] = one
        stat[1, f + nf : f + nf + 1] = two
        for row in range(hr):
            if f >= nf - 2 or row in (0, hr - 1):
                own2[f, row] = total[row // 2, :, (row % 2) * ch : (row % 2 + 1) * ch].astype(own2.dtype)

    def send_middle(first):
        sends = [
            send(own2.at[nf - 2 : nf, hr - 1], ext2.at[0:2, 0], first, after, below),
            send(own2.at[nf - 2 : nf, 0], ext2.at[0:2, hr + 1], first + 1, after, above),
            send(own2.at[nf - 2 : nf], ext2.at[0:2, 1 : 1 + hr], first + 2, after, r),
        ]
        for each in sends:
            each.start()
        return sends

    middle_done(3)
    middle_done(2)
    halos2 = send_middle(11)
    prev_affine(0)
    for halo in halos[2:]:
        halo.wait_recv()

    @pl.loop(0, 2)
    def _(s):
        permute(s, range(hr + 2))

    conv_prev(0)
    for f in (1, 0):
        middle_done(f)
    sum_start(1)
    edges2 = [
        send(own2.at[:, hr - 1], ext2.at[2 : 2 + nf, 0], 17, t, below),
        send(own2.at[:, 0], ext2.at[2 : 2 + nf, hr + 1], 18, t, above),
    ]
    for edge in edges2:
        edge.start()
    sum_middle(1)
    own_affine(1)
    for edge in edges2:
        edge.wait_recv()
    conv_own(1)

    def output_done(f):
        total = acc[f].reshape(pairs, wc, 2 * ch)
        for row in range(hr):
            piece = total[row // 2, :, (row % 2) * ch : (row % 2 + 1) * ch]
            for j in range(8):
                turn[row, pl.ds(j, 8, stride=8)] = piece[8 * j : 8 * j + 8]
            kept = ext[f + 2, row + 1].astype(jnp.float32)
            out[f, row] = (kept + turn[row]).astype(out.dtype)

    output_done(3)
    output_done(2)
    prev_affine(1)
    for halo in halos2:
        halo.wait_recv()
    conv_prev(1)
    for f in (1, 0):
        output_done(f)
    for sent in halos + halos2 + edges2:
        sent.wait_send()
    sum_drain(0)
    sum_drain(1)

def body(frames, video_pos, gain1, shift1, weight1, gain2, shift2, weight2):
    nt = lax.axis_size("tm")
    nr = lax.axis_size("rows")
    nf, hr, wc, ch = frames.shape
    near_n = near_size(nr)
    far_n = nr // near_n
    bf, f32 = jnp.bfloat16, jnp.float32
    hbm = pl.BlockSpec(memory_space=pltpu.HBM)
    call = pl.pallas_call(
        functools.partial(kernel, nt, nr),
        out_shape=pltpu.VMEM(frames.shape, frames.dtype),
        in_specs=[hbm] * 8,
        out_specs=pl.BlockSpec(memory_space=pltpu.VMEM),
        scratch_shapes=[
            pltpu.VMEM((nf + 2, hr + 2, wc, ch), bf),
            pltpu.VMEM((nf + 2, hr + 2, wc, ch), bf),
            pltpu.VMEM((nf, hr, wc, ch), bf),
            pltpu.VMEM((nf, hr // 2 * wc, 2 * ch), f32),
            pltpu.VMEM((nf + 2, hr // 2 + 1, wc, 6 * ch), bf),
            pltpu.VMEM((nf + 2, hr + 2, wc, ch), f32),
            pltpu.VMEM((hr + 2, wc, ch), f32),
            pltpu.VMEM((2, 27 * ch, ch), bf),
            pltpu.VMEM((2, 3, 12 * ch, 2 * ch), bf),
            pltpu.VMEM((4, 1, ch), f32),
            pltpu.SMEM((nf,), jnp.int32),
            pltpu.VMEM((2, 2, 2, 8, ch), f32),
            pltpu.VMEM((2, 2 * nf, ch), f32),
            pltpu.VMEM((2, 2, ch), f32),
            pltpu.VMEM((2, 2, ch), f32),
            pltpu.VMEM((2, near_n, 2, ch), f32),
            pltpu.VMEM((2, far_n, 2, ch), f32),
            pltpu.VMEM((2, far_n, 2, ch), f32),
            pltpu.SemaphoreType.DMA((12,)),
            pltpu.SemaphoreType.DMA((19,)),
            pltpu.SemaphoreType.DMA((19,)),
        ],
        compiler_params=pltpu.CompilerParams(
            collective_id=0, has_side_effects=True, vmem_limit_bytes=40 * 1024 * 1024
        ),
        name="encoder_block",
    )
    operands = (
        frames,
        video_pos,
        gain1.reshape(1, ch),
        shift1.reshape(1, ch),
        weight1.reshape(27 * ch, ch),
        gain2.reshape(1, ch),
        shift2.reshape(1, ch),
        weight2.reshape(27 * ch, ch),
    )
    return call(*(pltpu.with_memory_space_constraint(x, pltpu.HBM) for x in operands))


def solution(mesh):
    placed = (P("tm", "rows", None, None), P("tm"), P(), P(), P(), P(), P(), P())
    return jax.shard_map(
        body, mesh=mesh, in_specs=placed, out_specs=P("tm", "rows", None, None), check_vma=False
    )
```

```python
import functools

import jax
import jax.numpy as jnp
from jax import lax
from jax.experimental import pallas as pl
from jax.experimental.pallas import tpu as pltpu
from jax.sharding import PartitionSpec as P

GROUP = 4
EPS = 1e-06
MESH = pl.DeviceIdType.MESH


def near_size(rows):
    size = 1
    while size * size < rows:
        size *= 2
    return size


def kernel(
    nt,
    nr,
    frames,
    video_pos,
    gain1,
    shift1,
    weight1,
    gain2,
    shift2,
    weight2,
    out,
    ext,
    ext2,
    own2,
    acc,
    act,
    raw,
    turn,
    wraw,
    wpair,
    params,
    pos,
    affine,
    stat,
    packed,
    part,
    near,
    far,
    prev,
    load_sem,
    send_sem,
    recv_sem,
):
    nf, hr, wc, ch = frames.shape
    pairs = hr // 2
    near_n = near.shape[1]
    far_n = far.shape[1]
    count = float(nr * hr * wc * GROUP)
    t = lax.axis_index("tm")
    r = lax.axis_index("rows")
    in_near = lax.rem(r, near_n)
    in_far = lax.div(r, near_n)
    above = lax.rem(r + nr - 1, nr)
    below = lax.rem(r + 1, nr)
    after = lax.rem(t + 1, nt)
    before = lax.rem(t + nt - 1, nt)

    def far_first(n):
        return sorted(range(1, n), key=lambda step: -min(step, n - step))

    def near_peer(step):
        return in_far * near_n + lax.rem(in_near + step, near_n)

    def far_peer(step):
        return lax.rem(in_far + step, far_n) * near_n + in_near

    loads = [
        pltpu.make_async_copy(weight1, wraw.at[0], load_sem.at[1]),
        pltpu.make_async_copy(weight2, wraw.at[1], load_sem.at[2]),
        pltpu.make_async_copy(video_pos, pos, load_sem.at[3]),
        pltpu.make_async_copy(gain1, params.at[0], load_sem.at[4]),
        pltpu.make_async_copy(shift1, params.at[1], load_sem.at[5]),
        pltpu.make_async_copy(gain2, params.at[2], load_sem.at[6]),
        pltpu.make_async_copy(shift2, params.at[3], load_sem.at[7]),
    ]
    frame_loads = [
        pltpu.make_async_copy(frames.at[f], ext.at[f + 2, 1 : 1 + hr], load_sem.at[8 + f])
        for f in range(nf)
    ]
    for load in frame_loads:
        load.start()

    barrier = pltpu.get_barrier_semaphore()

    def greet(tt, rr):
        pl.semaphore_signal(barrier, inc=1, device_id=(tt, rr), device_id_type=MESH)

    for step in far_first(far_n):
        greet(t, far_peer(step))
    for step in far_first(near_n):
        greet(t, near_peer(step))
    for step in far_first(far_n) + [0]:
        greet(before, far_peer(step))

    greet(t, above)
    greet(t, below)
    greet(before, above)
    greet(before, below)

    for load in loads:
        load.start()

    def send(src, dst, which, tt, rr):
        return pltpu.make_async_remote_copy(
            src_ref=src,
            dst_ref=dst,
            send_sem=send_sem.at[which],
            recv_sem=recv_sem.at[which],
            device_id=(tt, rr),
            device_id_type=MESH,
        )

    lane = lax.broadcasted_iota(jnp.int32, (8, ch), 1)
    own_lane = lax.rem(lane, GROUP) == lax.rem(lax.broadcasted_iota(jnp.int32, (8, ch), 0), GROUP)

    def group_sums(x):
        for width in (1, 2):
            up = pltpu.roll(x, width, 1)
            down = pltpu.roll(x, ch - width, 1)
            x = x + jnp.where(lax.rem(lax.div(lane, width), 2) == 0, down, up)
        return x

    def sum_start(phase):
        own = jnp.where(own_lane, group_sums(stat[phase]), 0.0)
        one = jnp.sum(own[:nf], axis=0, keepdims=True)
        two = jnp.sum(own[nf:], axis=0, keepdims=True)
        packed[phase] = jnp.concatenate([one, two], axis=0)
        near[phase, in_near] = packed[phase]

        for step in far_first(near_n):
            send(
                packed.at[phase], near.at[phase, in_near], 3 * phase, t, near_peer(step)
            ).start()

    def wait_many(ref, sem):
        pltpu.make_async_copy(ref, ref, sem).wait()

    def sum_middle(phase):
        wait_many(near.at[phase, 0 : near_n - 1], recv_sem.at[3 * phase])
        total = jnp.sum(near[phase], axis=0)
        part[phase] = total
        far[phase, in_far] = total

        for step in far_first(far_n):
            send(
                part.at[phase], far.at[phase, in_far], 3 * phase + 1, t, far_peer(step)
            ).start()

        for step in far_first(far_n) + [0]:
            send(
                part.at[phase], prev.at[phase, in_far], 3 * phase + 2, after, far_peer(step)
            ).start()

    def sum_drain(phase):
        wait_many(near.at[phase, 0 : near_n - 1], send_sem.at[3 * phase])
        wait_many(far.at[phase, 0 : far_n - 1], send_sem.at[3 * phase + 1])
        wait_many(prev.at[phase], send_sem.at[3 * phase + 2])

    def set_affine(phase, total, at):
        sums = [
            group_sums(jnp.where(own_lane, jnp.broadcast_to(total[i : i + 1], (8, ch)), 0.0))
            for i in range(2)
        ]
        mean = sums[0] / count
        spread = sums[1] / count - mean * mean
        scale = lax.rsqrt(spread + EPS) * params[2 * phase]
        affine[phase, at, 0] = scale
        affine[phase, at, 1] = params[2 * phase + 1] - mean * scale

    def own_affine(phase):
        wait_many(far.at[phase, 0 : far_n - 1], recv_sem.at[3 * phase + 1])
        set_affine(phase, jnp.sum(far[phase], axis=0), 1)

    def prev_affine(phase):
        wait_many(prev.at[phase], recv_sem.at[3 * phase + 2])
        set_affine(phase, jnp.sum(prev[phase], axis=0), 0)

    def fill_weights(layer):
        zeros = jnp.zeros((3 * ch, ch), wpair.dtype)
        for k in range(3):
            for i in range(3):
                tap = wraw[layer, (3 * k + i) * 3 * ch : (3 * k + i + 1) * 3 * ch]
                for par in range(2):
                    u = i + par
                    wpair[layer, k, u * 3 * ch : (u + 1) * 3 * ch, par * ch : (par + 1) * ch] = tap
            wpair[layer, k, 9 * ch : 12 * ch, 0:ch] = zeros
            wpair[layer, k, 0 : 3 * ch, ch : 2 * ch] = zeros

    row_ok = (
        jnp.where(r > 0, 1.0, 0.0).astype(jnp.float32),
        jnp.where(r < nr - 1, 1.0, 0.0).astype(jnp.float32),
    )

    eight = lax.broadcasted_iota(jnp.int32, (8, ch), 0)

    def norm_row(x, phase, s, row, own):
        f = s - 2 if own else s + nf - 2
        y = x * affine[phase, int(own), 0, pl.ds(f, 1)] + affine[phase, int(own), 1, pl.ds(f, 1)]
        a = y * (0.5 * jnp.tanh(0.5 * y) + 0.5)
        if row == 0:
            a = a * row_ok[0]
        if row == hr + 1:
            a = a * row_ok[1]
        first = jnp.where(eight == 0, 0.0, pltpu.roll(a[wc - 8 :], 1, 0))
        last = jnp.where(eight == 7, 0.0, pltpu.roll(a[:8], 7, 0))
        lo = (row % 2) * 3 * ch
        act[s, row // 2, :, lo : lo + ch] = jnp.concatenate([first, a[: wc - 8]], axis=0).astype(act.dtype)
        act[s, row // 2, :, lo + ch : lo + 2 * ch] = a.astype(act.dtype)
        act[s, row // 2, :, lo + 2 * ch : lo + 3 * ch] = jnp.concatenate([a[8:], last], axis=0).astype(act.dtype)

    def permute(s, rows):
        for row in rows:
            turn[row] = ext[s, row].astype(jnp.float32)
            for j in range(8):
                raw[s, row, 8 * j : 8 * j + 8] = turn[row, pl.ds(j, 8, stride=8)]

    def norm_frame(phase, s, own):
        for row in range(hr + 2):
            if phase == 0:
                x = raw[s, row]
            elif not own or row in (0, hr + 1):
                x = ext2[s, row].astype(jnp.float32)
            else:
                q = row - 1
                x = acc[s - 2, (q // 2) * wc : (q // 2 + 1) * wc, (q % 2) * ch : (q % 2 + 1) * ch]
            norm_row(x, phase, s, row, own)

    def product(layer, s, w):
        lhs = jnp.concatenate(
            [act[s, half : half + pairs].reshape(pairs * wc, 6 * ch) for half in range(2)], axis=1
        )
        return jnp.dot(lhs, wpair[layer, w], preferred_element_type=jnp.float32)

    def source(f, k):
        return f + 2 - jnp.minimum(2 - k, pos[f])

    def conv_own(layer):
        norm_frame(layer, 5, True)
        acc[3] = product(layer, 5, 2)
        norm_frame(layer, 4, True)
        acc[3] = acc[3] + product(layer, 4, 1)
        acc[2] = product(layer, 4, 2)
        norm_frame(layer, 3, True)
        acc[1] = product(layer, 3, 2)
        norm_frame(layer, 2, True)
        acc[0] = product(layer, 2, 2)
        acc[3] = acc[3] + product(layer, source(3, 0), 0)
        acc[2] = acc[2] + product(layer, source(2, 1), 1) + product(layer, source(2, 0), 0)
        acc[1] = acc[1] + product(layer, source(1, 1), 1)

    def conv_prev(layer):
        norm_frame(layer, 1, False)
        acc[1] = acc[1] + product(layer, source(1, 0), 0)
        norm_frame(layer, 0, False)
        acc[0] = acc[0] + product(layer, source(0, 1), 1) + product(layer, source(0, 0), 0)

    def column_sums(x):
        return jnp.sum(x, axis=0, keepdims=True)

    for f in range(nf):
        frame_loads[f].wait()
        one = jnp.zeros((8, ch), jnp.float32)
        two = jnp.zeros((8, ch), jnp.float32)
        for row in range(1, hr + 1):
            x = ext[f + 2, row].astype(jnp.float32).reshape(wc // 8, 8, ch)
            one = one + jnp.sum(x, axis=0)
            two = two + jnp.sum(x * x, axis=0)
        stat[0, f : f + 1] = column_sums(one)
        stat[0, f + nf : f + nf + 1] = column_sums(two)

    pl.semaphore_wait(barrier, near_n - 1 + 2 * far_n - 1 + 4)
    sum_start(0)

    halos = [
        send(frames.at[:, hr - 1], ext.at[2 : 2 + nf, 0], 6, t, below),
        send(frames.at[:, 0], ext.at[2 : 2 + nf, hr + 1], 7, t, above),
        send(frames.at[nf - 2 : nf, hr - 1], ext.at[0:2, 0], 8, after, below),
        send(frames.at[nf - 2 : nf, 0], ext.at[0:2, hr + 1], 9, after, above),
        send(frames.at[nf - 2 : nf], ext.at[0:2, 1 : 1 + hr], 10, after, r),
    ]
    for halo in halos:
        halo.start()

    loads[0].wait()
    fill_weights(0)

    @pl.loop(2, 2 + nf)
    def _(s):
        permute(s, range(1, 1 + hr))

    sum_middle(0)
    loads[1].wait()
    fill_weights(1)
    for load in loads[2:]:
        load.wait()
    halos[0].wait_recv()
    halos[1].wait_recv()

    @pl.loop(2, 2 + nf)
    def _(s):
        permute(s, (0, hr + 1))

    own_affine(0)
    conv_own(0)

    def middle_done(f):
        total = acc[f].reshape(pairs, wc, 2 * ch)
        one = jnp.sum(total.reshape(pairs * wc // 8, 8, 2 * ch), axis=0)
        two = jnp.sum((total * total).reshape(pairs * wc // 8, 8, 2 * ch), axis=0)
        one = column_sums(one[:, :ch] + one[:, ch:])
        two = column_sums(two[:, :ch] + two[:, ch:])
        stat[1, f : f + 1] = one
        stat[1, f + nf : f + nf + 1] = two
        for row in range(hr):
            if f >= nf - 2 or row in (0, hr - 1):
                own2[f, row] = total[row // 2, :, (row % 2) * ch : (row % 2 + 1) * ch].astype(own2.dtype)

    def send_middle(first):
        sends = [
            send(own2.at[nf - 2 : nf, hr - 1], ext2.at[0:2, 0], first, after, below),
            send(own2.at[nf - 2 : nf, 0], ext2.at[0:2, hr + 1], first + 1, after, above),
            send(own2.at[nf - 2 : nf], ext2.at[0:2, 1 : 1 + hr], first + 2, after, r),
        ]
        for each in sends:
            each.start()
        return sends

    middle_done(3)
    middle_done(2)
    halos2 = send_middle(11)
    prev_affine(0)
    for halo in halos[2:]:
        halo.wait_recv()

    @pl.loop(0, 2)
    def _(s):
        permute(s, range(hr + 2))

    conv_prev(0)
    for f in (1, 0):
        middle_done(f)
    sum_start(1)
    edges2 = [
        send(own2.at[:, hr - 1], ext2.at[2 : 2 + nf, 0], 17, t, below),
        send(own2.at[:, 0], ext2.at[2 : 2 + nf, hr + 1], 18, t, above),
    ]
    for edge in edges2:
        edge.start()
    sum_middle(1)
    own_affine(1)
    for edge in edges2:
        edge.wait_recv()
    conv_own(1)

    def output_done(f):
        total = acc[f].reshape(pairs, wc, 2 * ch)
        for row in range(hr):
            piece = total[row // 2, :, (row % 2) * ch : (row % 2 + 1) * ch]
            for j in range(8):
                turn[row, pl.ds(j, 8, stride=8)] = piece[8 * j : 8 * j + 8]
            kept = ext[f + 2, row + 1].astype(jnp.float32)
            out[f, row] = (kept + turn[row]).astype(out.dtype)

    output_done(3)
    output_done(2)
    prev_affine(1)
    for halo in halos2:
        halo.wait_recv()
    conv_prev(1)
    for f in (1, 0):
        output_done(f)
    for sent in halos + halos2 + edges2:
        sent.wait_send()
    sum_drain(0)
    sum_drain(1)

def body(frames, video_pos, gain1, shift1, weight1, gain2, shift2, weight2):
    nt = lax.axis_size("tm")
    nr = lax.axis_size("rows")
    nf, hr, wc, ch = frames.shape
    near_n = near_size(nr)
    far_n = nr // near_n
    bf, f32 = jnp.bfloat16, jnp.float32
    hbm = pl.BlockSpec(memory_space=pltpu.HBM)
    call = pl.pallas_call(
        functools.partial(kernel, nt, nr),
        out_shape=pltpu.VMEM(frames.shape, frames.dtype),
        in_specs=[hbm] * 8,
        out_specs=pl.BlockSpec(memory_space=pltpu.VMEM),
        scratch_shapes=[
            pltpu.VMEM((nf + 2, hr + 2, wc, ch), bf),
            pltpu.VMEM((nf + 2, hr + 2, wc, ch), bf),
            pltpu.VMEM((nf, hr, wc, ch), bf),
            pltpu.VMEM((nf, hr // 2 * wc, 2 * ch), f32),
            pltpu.VMEM((nf + 2, hr // 2 + 1, wc, 6 * ch), bf),
            pltpu.VMEM((nf + 2, hr + 2, wc, ch), f32),
            pltpu.VMEM((hr + 2, wc, ch), f32),
            pltpu.VMEM((2, 27 * ch, ch), bf),
            pltpu.VMEM((2, 3, 12 * ch, 2 * ch), bf),
            pltpu.VMEM((4, 1, ch), f32),
            pltpu.SMEM((nf,), jnp.int32),
            pltpu.VMEM((2, 2, 2, 8, ch), f32),
            pltpu.VMEM((2, 2 * nf, ch), f32),
            pltpu.VMEM((2, 2, ch), f32),
            pltpu.VMEM((2, 2, ch), f32),
            pltpu.VMEM((2, near_n, 2, ch), f32),
            pltpu.VMEM((2, far_n, 2, ch), f32),
            pltpu.VMEM((2, far_n, 2, ch), f32),
            pltpu.SemaphoreType.DMA((12,)),
            pltpu.SemaphoreType.DMA((19,)),
            pltpu.SemaphoreType.DMA((19,)),
        ],
        compiler_params=pltpu.CompilerParams(
            collective_id=0, has_side_effects=True, vmem_limit_bytes=40 * 1024 * 1024
        ),
        name="encoder_block",
    )
    operands = (
        frames,
        video_pos,
        gain1.reshape(1, ch),
        shift1.reshape(1, ch),
        weight1.reshape(27 * ch, ch),
        gain2.reshape(1, ch),
        shift2.reshape(1, ch),
        weight2.reshape(27 * ch, ch),
    )
    return call(*(pltpu.with_memory_space_constraint(x, pltpu.HBM) for x in operands))


def solution(mesh):
    placed = (P("tm", "rows", None, None), P("tm"), P(), P(), P(), P(), P(), P())
    return jax.shard_map(
        body, mesh=mesh, in_specs=placed, out_specs=P("tm", "rows", None, None), check_vma=False
    )
```
